32 devices in a mesh: dp: 2 (over core), seq: 4 (over z), tensor: 4 (over y, x).
Axes of the slice: x: 2, y: 2, z: 4, core: 2. Of those that a mesh axis runs over, the one named last changes fastest.
Arguments:
- tokens: bfloat16 [2, 2048, 1024], P('dp', 'seq'), may hold values from -6 to 6
- cotangent: bfloat16 [2, 2048, 1024], P('dp', 'seq'), may hold values from -6 to 6
- attention_gain: bfloat16 [1024], replicated, may hold values from 0.5 to 1.5
- query_proj: bfloat16 [1024, 512], P(None, 'tensor'), may hold values from -0.1875 to 0.1875
- key_proj: bfloat16 [1024, 512], P(None, 'tensor'), may hold values from -0.1875 to 0.1875
- value_proj: bfloat16 [1024, 1024], P(None, 'tensor'), may hold values from -0.1875 to 0.1875
- query_conv: bfloat16 [4, 512], P(None, 'tensor'), may hold values from -3 to 3
- key_conv: bfloat16 [4, 512], P(None, 'tensor'), may hold values from -3 to 3
- value_conv: bfloat16 [4, 1024], P(None, 'tensor'), may hold values from -3 to 3
- decay_down: bfloat16 [1024, 16], replicated, may hold values from -0.1875 to 0.1875
- decay_up: bfloat16 [16, 512], P(None, 'tensor'), may hold values from -2 to 2
- decay_bias: float32 [512], P('tensor'), may hold values from 0.3 to 10
- swish_proj: bfloat16 [1024, 1024], P(None, 'tensor'), may hold values from -0.1875 to 0.1875
- head_gain: bfloat16 [256], replicated, may hold values from 0.5 to 1.5
- output_proj: bfloat16 [1024, 1024], P('tensor'), may hold values from -0.25 to 0.25
- feed_gain: bfloat16 [1024], replicated, may hold values from 0.5 to 1.5
- feed_gate: bfloat16 [1024, 2816], P(None, 'tensor'), may hold values from -0.1875 to 0.1875
- feed_lift: bfloat16 [1024, 2816], P(None, 'tensor'), may hold values from -0.1875 to 0.1875
- feed_down: bfloat16 [2816, 1024], P('tensor'), may hold values from -0.21875 to 0.21875
Outputs:
- mixed: bfloat16 [2, 2048, 1024], P('dp', 'seq')
- tokens_grad: float32 [2, 2048, 1024], P('dp', 'seq')
- grad_attention_gain: float32 [1024], replicated
- grad_query_proj: float32 [1024, 512], P(None, 'tensor')
- grad_key_proj: float32 [1024, 512], P(None, 'tensor')
- grad_value_proj: float32 [1024, 1024], P(None, 'tensor')
- grad_query_conv: float32 [4, 512], P(None, 'tensor')
- grad_key_conv: float32 [4, 512], P(None, 'tensor')
- grad_value_conv: float32 [4, 1024], P(None, 'tensor')
- grad_decay_down: float32 [1024, 16], replicated
- grad_decay_up: float32 [16, 512], P(None, 'tensor')
- grad_decay_bias: float32 [512], P('tensor')
- grad_swish_proj: float32 [1024, 1024], P(None, 'tensor')
- grad_head_gain: float32 [256], replicated
- grad_output_proj: float32 [1024, 1024], P('tensor')
- grad_feed_gain: float32 [1024], replicated
- grad_feed_gate: float32 [1024, 2816], P(None, 'tensor')
- grad_feed_lift: float32 [1024, 2816], P(None, 'tensor')
- grad_feed_down: float32 [2816, 1024], P('tensor')
The draws below stay inside these ranges and needn't reach their ends.
All inputs are finite; a program needn't handle non-finite values.
Results may differ from the reference program's by a relative error of at most 0.017.
The reference program's roundings to bfloat16 on the way count: a program that leaves them out, or rounds other values in their place, can miss the bound.
Values may be sent and summed in bfloat16 or wider, within the bound.
A program may use at most 128 MiB of HBM per device.

```python
import math
import jax
import jax.numpy as jnp
from jax import lax

D = 1024
HEADS = 4
HEAD_KEY = 128
HEAD_VALUE = 256
RANK = 16
FF = 2816
CONV = 4
SPAN = 64
SEQS = 2
LENGTH = 2048
KEYS = 512
VALS = 1024


def draw_decay_bias(key, part):
    key = jax.random.fold_in(key, 11)
    pick_key, slow_key, fast_key = jax.random.split(key, 3)
    slow_share = 0.5
    slow_mask = jax.random.uniform(pick_key, (KEYS,)) < slow_share
    slow_rate = jnp.exp(jax.random.uniform(slow_key, (KEYS,), minval=math.log(0.1), maxval=0.0)) * (math.log(10.0) / LENGTH)
    fast_rate = jnp.exp(jax.random.uniform(fast_key, (KEYS,), minval=math.log(1.0 / 50.0), maxval=math.log(1.0 / 30.0)))
    rate = jnp.where(slow_mask, slow_rate, fast_rate)
    return (-jnp.log(jnp.expm1(16.0 * rate))).astype(jnp.float32)


def levels(key, dims, cuts, low, largest):
    level, own = 1.0, jax.random.fold_in(key, 6)
    for position, shards_of in cuts:
        draws = jnp.exp(jax.random.uniform(jax.random.fold_in(own, position), (shards_of,), jnp.float32, low / len(cuts), largest / len(cuts)))
        level = level * jnp.repeat(draws, dims[position] // shards_of).reshape([-1 if axis == position else 1 for axis in range(len(dims))])
    return level


def noise(own_key, shape, scale, limit, pieces=(), held_as=jnp.bfloat16):
    level = levels(own_key, shape, pieces, -0.22, 0.18) if pieces else 1.0
    values = jax.random.normal(own_key, shape, jnp.float32) * scale * level
    return jnp.minimum(jnp.maximum(values, -limit), limit).astype(held_as)


def setup_inputs(seed: int = 0) -> dict:
    arg_keys = jax.random.split(jax.random.key(seed), 20)
    return {
        "tokens": noise(arg_keys[0], (SEQS, LENGTH, D), 1.0, 6.0, ((0, 2), (1, 4))),
        "cotangent": noise(arg_keys[1], (SEQS, LENGTH, D), 1.0, 6.0, ((0, 2), (1, 4))),
        "attention_gain": jnp.clip(1.0 + 0.1 * jax.random.normal(arg_keys[2], (D,), jnp.float32), 0.5, 1.5).astype(jnp.bfloat16),
        "query_proj": noise(arg_keys[3], (D, KEYS), D ** -0.5, 0.1875, ((1, 4),)),
        "key_proj": noise(arg_keys[4], (D, KEYS), D ** -0.5, 0.1875, ((1, 4),)),
        "value_proj": noise(arg_keys[5], (D, VALS), D ** -0.5, 0.1875, ((1, 4),)),
        "query_conv": noise(arg_keys[6], (CONV, KEYS), CONV ** -0.5, 3.0, ((1, 4),)),
        "key_conv": noise(arg_keys[7], (CONV, KEYS), CONV ** -0.5, 3.0, ((1, 4),)),
        "value_conv": noise(arg_keys[8], (CONV, VALS), CONV ** -0.5, 3.0, ((1, 4),)),
        "decay_down": noise(arg_keys[9], (D, RANK), D ** -0.5, 0.1875),
        "decay_up": noise(arg_keys[10], (RANK, KEYS), (0.5 * RANK ** -0.5), 2.0, ((1, 4),)),
        "decay_bias": draw_decay_bias(jax.random.fold_in(arg_keys[19], 71), 0),
        "swish_proj": noise(arg_keys[12], (D, VALS), D ** -0.5, 0.1875, ((1, 4),)),
        "head_gain": jnp.clip(1.0 + 0.1 * jax.random.normal(arg_keys[13], (HEAD_VALUE,), jnp.float32), 0.5, 1.5).astype(jnp.bfloat16),
        "output_proj": noise(arg_keys[14], (VALS, D), (VALS // 2) ** -0.5, 0.25, ((0, 4),)),
        "feed_gain": jnp.clip(1.0 + 0.1 * jax.random.normal(arg_keys[15], (D,), jnp.float32), 0.5, 1.5).astype(jnp.bfloat16),
        "feed_gate": noise(arg_keys[16], (D, FF), D ** -0.5, 0.1875, ((1, 4),)),
        "feed_lift": noise(arg_keys[17], (D, FF), D ** -0.5, 0.1875, ((1, 4),)),
        "feed_down": noise(arg_keys[18], (FF, D), (FF // 4) ** -0.5, 0.21875, ((0, 4),)),
    }


highest = lax.Precision.HIGHEST
epsilon = 1e-06

@jax.custom_vjp
def low(v):
    return lax.optimization_barrier(v.astype(jnp.bfloat16)).astype(jnp.float32)

@jax.custom_vjp
def low_back(v):
    return v

def low_keep(v):
    return (low(v), None)

def low_pass(kept, grad):
    return (grad,)

def back_keep(v):
    return (v, None)

def back_low(kept, grad):
    return (low(grad),)
low.defvjp(low_keep, low_pass)
low_back.defvjp(back_keep, back_low)

def root_norm(values, gain):
    return values * lax.rsqrt(lax.optimization_barrier(jnp.mean(values * values, axis=-1, keepdims=True)) + epsilon) * gain

def project(left, right):
    return jnp.einsum('...d,de->...e', left, right, precision=highest)

def convolve(padded, weight):
    width = weight.shape[0]
    length = padded.shape[1] - width + 1
    total = weight[0] * padded[:, 0:length]
    for offset in range(1, width):
        total = total + weight[offset] * padded[:, offset:offset + length]
    return jax.nn.silu(total)

def block_step(memory, block):
    queries, keylist, values, decays = block
    extent = queries.shape[1]
    cumul = jnp.cumsum(decays, axis=1)
    causal = (jnp.arange(extent)[:, None] >= jnp.arange(extent)[None, :])[None, :, :, None]
    spread = cumul[:, :, None, :] - cumul[:, None, :, :]
    weights = jnp.where(causal, jnp.exp(jnp.where(causal, spread, 0.0)), 0.0)
    scores = jnp.einsum('ntd,nsd,ntsd->nts', queries, keylist, weights, precision=highest)
    inner = jnp.einsum('nts,nse->nte', scores, values, precision=highest)
    carried = jnp.einsum('ntd,nde->nte', queries * jnp.exp(cumul), memory, precision=highest)
    ending = cumul[:, -1:, :]
    fresh = jnp.einsum('nsd,nse->nde', keylist * jnp.exp(ending - cumul), values, precision=highest)
    return (jnp.exp(ending[:, 0, :])[:, :, None] * memory + fresh, inner + carried)

def recurrence(queries, keylist, values, decays, memory):
    groups, length, _ = queries.shape
    blocks = length // SPAN

    def split_blocks(array):
        return jnp.moveaxis(array.reshape(groups, blocks, SPAN, array.shape[-1]), 1, 0)
    memory, outputs = lax.scan(jax.checkpoint(block_step), memory, (split_blocks(queries), split_blocks(keylist), split_blocks(values), split_blocks(decays)))
    return (jnp.moveaxis(outputs, 0, 1).reshape(groups, length, -1), memory)

def to_heads(array, width):
    batch, length, channels = array.shape
    return array.reshape(batch, length, channels // width, width).transpose(0, 2, 1, 3).reshape(batch * (channels // width), length, width)

def from_heads(array, batch):
    groups, length, width = array.shape
    return array.reshape(batch, groups // batch, length, width).transpose(0, 2, 1, 3).reshape(batch, length, groups // batch * width)

def forward(tokens, attention_gain, query_proj, key_proj, value_proj, query_conv, key_conv, value_conv, decay_down, decay_up, decay_bias, swish_proj, head_gain, output_proj, feed_gain, feed_gate, feed_lift, feed_down):
    batch = tokens.shape[0]
    hidden = low(root_norm(tokens, attention_gain))
    pads = ((0, 0), (CONV - 1, 0), (0, 0))
    query_raw = low_back(low(project(hidden, query_proj)))
    key_raw = low_back(low(project(hidden, key_proj)))
    value_raw = low_back(low(project(hidden, value_proj)))
    queries = convolve(jnp.pad(query_raw, pads), query_conv) * HEAD_KEY ** (-0.5)
    keylist = convolve(jnp.pad(key_raw, pads), key_conv)
    values = convolve(jnp.pad(value_raw, pads), value_conv)
    low_rank = project(hidden, decay_down)
    decay_logit = project(low_rank, decay_up) + decay_bias
    log_decay = jax.nn.log_sigmoid(decay_logit) / 16.0
    heads_q = to_heads(queries, HEAD_KEY)
    start = jnp.zeros((heads_q.shape[0], HEAD_KEY, HEAD_VALUE), jnp.float32)
    recurrent, _ = recurrence(heads_q, to_heads(keylist, HEAD_KEY), to_heads(values, HEAD_VALUE), to_heads(log_decay, HEAD_KEY), start)
    recurrent = from_heads(recurrent, batch).reshape(batch, -1, HEADS, HEAD_VALUE)
    swish_gate = low_back(project(hidden, swish_proj)).reshape(batch, -1, HEADS, HEAD_VALUE)
    gated = low(root_norm(recurrent, head_gain) * jax.nn.silu(swish_gate)).reshape(batch, -1, VALS)
    middle = tokens + low_back(project(gated, output_proj))
    hidden_two = low(root_norm(middle, feed_gain))
    gate_pre = low_back(project(hidden_two, feed_gate))
    lift_pre = low_back(project(hidden_two, feed_lift))
    activation = low(jax.nn.silu(gate_pre) * lift_pre)
    return middle + low_back(project(activation, feed_down))

def reference(tokens, cotangent, attention_gain, query_proj, key_proj, value_proj, query_conv, key_conv, value_conv, decay_down, decay_up, decay_bias, swish_proj, head_gain, output_proj, feed_gain, feed_gate, feed_lift, feed_down):
    primal = [tokens, attention_gain, query_proj, key_proj, value_proj, query_conv, key_conv, value_conv, decay_down, decay_up, decay_bias, swish_proj, head_gain, output_proj, feed_gain, feed_gate, feed_lift, feed_down]
    primal = [array.astype(jnp.float32) for array in primal]
    result, pullback = jax.vjp(forward, *primal)
    grads = pullback(cotangent.astype(jnp.float32))
    return (result.astype(jnp.bfloat16), grads[0], grads[1], grads[2], grads[3], grads[4], grads[5], grads[6], grads[7], grads[8], grads[9], grads[10], grads[11], grads[12], grads[13], grads[14], grads[15], grads[16], grads[17])
```

```python
import jax
import jax.numpy as jnp
import numpy as np
from jax import lax
from jax.experimental import pallas as pl
from jax.experimental.pallas import tpu as pltpu
from jax.sharding import PartitionSpec as P

HEAD_KEY = 128
CHUNK = 128


highest = lax.Precision.HIGHEST
epsilon = 1e-06


def shifted(x, axis, by):
    size = lax.axis_size(axis)
    pairs = [(i, i + by) for i in range(size) if 0 <= i + by < size]
    return lax.ppermute(x, axis, pairs)


def root_norm(values, gain):
    return values * lax.rsqrt(jnp.mean(values * values, axis=-1, keepdims=True) + epsilon) * gain


def convolve(padded, weight):
    width = weight.shape[0]
    length = padded.shape[1] - width + 1
    total = weight[0] * padded[:, 0:length]
    for offset in range(1, width):
        total = total + weight[offset] * padded[:, offset : offset + length]
    return jax.nn.silu(total)


def level_rows(chunk):
    index = np.arange(chunk)
    t, u = index[:, None], index[None, :]
    parts = []
    for level in range(chunk.bit_length() - 1):
        half = 1 << level
        last = (t // (2 * half)) * 2 * half + half - 1
        upper = (t > last) & (u > last) & (u <= t)
        lower = (t <= last) & (u > t) & (u <= last)
        parts.append(upper | lower)
    parts.append(u <= t)
    parts.append(u > t)
    return np.concatenate(parts, 0).astype(np.float32)


def dot(a, b, ca=1, cb=0):
    return lax.dot_general(
        a.astype(jnp.bfloat16),
        b.astype(jnp.bfloat16),
        (((ca,), (cb,)), ((), ())),
        preferred_element_type=jnp.float32,
    )


def chunk_factors(rows, decays):
    top = decays.astype(jnp.bfloat16)
    rest = (decays - top.astype(jnp.float32)).astype(jnp.bfloat16)
    both = dot(rows, jnp.concatenate([top, rest], 1))
    return both[:, :HEAD_KEY] + both[:, HEAD_KEY:]


def grids(chunk):
    t = lax.broadcasted_iota(jnp.int32, (chunk, chunk), 0)
    s = lax.broadcasted_iota(jnp.int32, (chunk, chunk), 1)
    r = lax.broadcasted_iota(jnp.int32, (chunk, HEAD_KEY), 0)
    return t, s, r


def chunk_scores(queries, keylist, factors, t, s, r, levels):
    chunk = queries.shape[0]
    mixed = t ^ s
    scores = jnp.where(
        t == s, jnp.sum(queries * keylist, axis=1, keepdims=True), 0.0
    )
    sides = []
    for level in range(levels):
        factor = factors[level * chunk : (level + 1) * chunk]
        side = (jnp.where(((r >> level) & 1) == 1, queries, keylist) * factor).astype(jnp.bfloat16)
        sides.append(side)
        product = dot(side, side, 1, 1)
        scores = jnp.where(((mixed >> level) == 1) & (t > s), product, scores)
    return scores, sides


def forward_kernel(rows_ref, q_ref, k_ref, v_ref, g_ref, o_ref, dq_ref, st_ref, off_ref, last_ref):
    chunk = rows_ref.shape[1]
    count = q_ref.shape[1] // chunk
    levels = chunk.bit_length() - 1
    rows = rows_ref[...]
    t, s, r = grids(chunk)
    state = jnp.zeros((v_ref.shape[2], HEAD_KEY), jnp.float32)
    offset = jnp.zeros((1, HEAD_KEY), jnp.float32)
    for c in range(count):
        part = pl.ds(c * chunk, chunk)
        queries, keylist, values = q_ref[0, part], k_ref[0, part], v_ref[0, part]
        raw = chunk_factors(rows, g_ref[0, part])
        factors = jnp.exp(raw)
        pre = factors[levels * chunk : (levels + 1) * chunk]
        suf = factors[(levels + 1) * chunk :]
        scores, _ = chunk_scores(queries, keylist, factors, t, s, r, levels)
        st_ref[0, c] = state
        off_ref[0, c] = jnp.broadcast_to(offset, (8, HEAD_KEY))
        queries_pre = queries * pre
        o_ref[0, part] = dot(scores, values) + dot(queries_pre, state, 1, 1)
        dq_ref[0, part] = queries_pre * jnp.exp(offset)
        state = state * pre[chunk - 1 :] + dot(values, keylist * suf, 0, 0)
        offset = offset + raw[(levels + 1) * chunk - 1 : (levels + 1) * chunk]
    off_ref[0, count] = jnp.broadcast_to(offset, (8, HEAD_KEY))
    last_ref[0] = state


def backward_kernel(
    rows_ref, rowst_ref, q_ref, k_ref, v_ref, g_ref, do_ref, st_ref, off_ref, inc_ref, out_ref,
    dq_ref, dk_ref, dv_ref, dg_ref,
):
    chunk = rows_ref.shape[1]
    count = q_ref.shape[1] // chunk
    levels = chunk.bit_length() - 1
    rows = rows_ref[...]
    rowst = rowst_ref[...]
    t, s, r = grids(chunk)
    mixed = t ^ s
    pull = out_ref[0]
    incoming = inc_ref[0]
    for c in reversed(range(count)):
        part = pl.ds(c * chunk, chunk)
        queries, keylist, values = q_ref[0, part], k_ref[0, part], v_ref[0, part]
        outer = do_ref[0, part]
        factors = jnp.exp(chunk_factors(rows, g_ref[0, part]))
        pre = factors[levels * chunk : (levels + 1) * chunk]
        suf = factors[(levels + 1) * chunk :]
        scores, sides = chunk_scores(queries, keylist, factors, t, s, r, levels)
        state = st_ref[0, c] + incoming * jnp.exp(off_ref[0, c][:1])
        lower = dot(outer, values, 1, 1)
        upper = dot(values, outer, 1, 1)
        both = jnp.where(t > s, lower, upper)
        own = jnp.sum(outer * values, axis=1, keepdims=True)
        dq = own * keylist
        dk = own * queries
        shares = []
        for level in range(levels):
            factor = factors[level * chunk : (level + 1) * chunk]
            back = dot(jnp.where((mixed >> level) == 1, both, 0.0), sides[level]) * factor
            bit = ((r >> level) & 1) == 1
            dq = dq + jnp.where(bit, back, 0.0)
            dk = dk + jnp.where(bit, 0.0, back)
            shares.append((back * jnp.where(bit, queries, keylist)).astype(jnp.bfloat16))
        from_state = dot(outer, state) * pre
        to_state = dot(values, pull) * suf
        dq = dq + from_state
        dk = dk + to_state
        shares.append((from_state * queries).astype(jnp.bfloat16))
        shares.append((to_state * keylist).astype(jnp.bfloat16))
        ending = pre[chunk - 1 :]
        whole = jnp.sum(state * pull, axis=0, keepdims=True) * ending
        dg = dot(rowst, jnp.concatenate(shares, 0)) + whole
        dq_ref[0, part] = dq
        dk_ref[0, part] = dk
        dg_ref[0, part] = dg
        dv_ref[0, part] = dot(scores, outer, 0, 0) + dot(keylist * suf, pull, 1, 1)
        pull = pull * ending + dot(outer, queries * pre, 0, 0)


def group_spec(shape):
    extra = len(shape) - 1
    return pl.BlockSpec((1,) + tuple(shape[1:]), lambda i: (i,) + (0,) * extra)


def whole_spec(shape):
    return pl.BlockSpec(tuple(shape), lambda i: (0,) * len(shape))


def run_groups(kernel, constants, arrays, outs, flops):
    return pl.pallas_call(
        kernel,
        grid=(arrays[0].shape[0],),
        in_specs=[whole_spec(a.shape) for a in constants] + [group_spec(a.shape) for a in arrays],
        out_specs=[group_spec(o) for o in outs],
        out_shape=[jax.ShapeDtypeStruct(o, jnp.float32) for o in outs],
        compiler_params=pltpu.CompilerParams(vmem_limit_bytes=48 * 1024 * 1024),
        cost_estimate=pl.CostEstimate(flops=flops, bytes_accessed=4000000, transcendentals=0),
    )(*constants, *arrays)


def state_chain(states, totals, order, me):
    carried = jnp.zeros_like(states[0])
    for j in order:
        follow = (j < me) if order[0] == 0 else (j > me)
        carried = jnp.where(follow, jnp.exp(totals[j]) * carried + states[j], carried)
    return carried


def to_heads(array, width):
    batch, length, channels = array.shape
    return (
        array.reshape(batch, length, channels // width, width)
        .transpose(0, 2, 1, 3)
        .reshape(batch * (channels // width), length, width)
    )


def from_heads(array, batch):
    groups, length, width = array.shape
    return (
        array.reshape(batch, groups // batch, length, width)
        .transpose(0, 2, 1, 3)
        .reshape(batch, length, groups // batch * width)
    )


def head_piece(outputs, gate, gain):
    return root_norm(outputs, gain) * jax.nn.silu(gate)


def feed_piece(gate_pre, lift_pre):
    return jax.nn.silu(gate_pre) * lift_pre


def split_sum(grads):
    sums = lax.psum(tuple(g.astype(jnp.bfloat16) for g in grads), ("dp", "seq"))
    return tuple(g.astype(jnp.float32) for g in sums)


def on_device(
    tokens,
    cotangent,
    attention_gain,
    query_proj,
    key_proj,
    value_proj,
    query_conv,
    key_conv,
    value_conv,
    decay_down,
    decay_up,
    decay_bias,
    swish_proj,
    head_gain,
    output_proj,
    feed_gain,
    feed_gate,
    feed_lift,
    feed_down,
):
    batch, seglen, width = tokens.shape
    rows = batch * seglen
    key_width = query_proj.shape[1]
    value_width = value_proj.shape[1]
    head_value = head_gain.shape[0]
    conv_width = query_conv.shape[0]
    scale = HEAD_KEY ** (-0.5)
    inputs_flat = tokens.astype(jnp.float32).reshape(rows, width)
    attention_gain_f = attention_gain.astype(jnp.float32)
    feed_gain_f = feed_gain.astype(jnp.float32)
    hidden_f, norm_back = jax.vjp(root_norm, inputs_flat, attention_gain_f)
    hidden = hidden_f.astype(jnp.bfloat16)
    query_raw = jnp.dot(hidden, query_proj, preferred_element_type=jnp.float32).astype(jnp.bfloat16)
    key_raw = jnp.dot(hidden, key_proj, preferred_element_type=jnp.float32).astype(jnp.bfloat16)
    value_raw = jnp.dot(hidden, value_proj, preferred_element_type=jnp.float32).astype(jnp.bfloat16)
    raw_rows = jnp.concatenate([query_raw, key_raw, value_raw], 1).reshape(batch, seglen, -1)
    edge_rows = shifted(raw_rows[:, seglen - conv_width + 1 :], "seq", 1)
    padded = jnp.concatenate([edge_rows, raw_rows], 1).astype(jnp.float32)
    conv_all = jnp.concatenate([query_conv, key_conv, value_conv], 1).astype(jnp.float32)
    activated, conv_back = jax.vjp(convolve, padded, conv_all)
    queries = to_heads(activated[..., :key_width] * scale, HEAD_KEY)
    keylist = to_heads(activated[..., key_width : 2 * key_width], HEAD_KEY)
    values = to_heads(activated[..., 2 * key_width :], head_value)
    low_rank = jnp.dot(hidden, decay_down, preferred_element_type=jnp.float32)
    decay_logit = jnp.dot(low_rank, decay_up.astype(jnp.float32), precision=highest) + decay_bias
    log_decay = jax.nn.log_sigmoid(decay_logit) / 16.0
    decays = to_heads(log_decay.reshape(batch, seglen, key_width), HEAD_KEY)
    groups = queries.shape[0]
    chunk = min(CHUNK, seglen)
    count = seglen // chunk
    row_table = level_rows(chunk)
    rows_const = jnp.asarray(row_table, jnp.bfloat16)
    rowst_const = jnp.asarray(row_table.T, jnp.bfloat16)
    flops = groups * seglen * 3000000
    local_out, decayed_q, states, offsets, local_state = run_groups(
        forward_kernel,
        (rows_const,),
        (queries, keylist, values, decays),
        (
            (groups, seglen, head_value),
            (groups, seglen, HEAD_KEY),
            (groups, count, head_value, HEAD_KEY),
            (groups, count + 1, 8, HEAD_KEY),
            (groups, head_value, HEAD_KEY),
        ),
        flops,
    )
    seq_size = lax.axis_size("seq")
    seq_me = lax.axis_index("seq")
    gathered = lax.all_gather(
        jnp.concatenate([local_state, offsets[:, count]], 1), "seq"
    )
    totals = gathered[:, :, head_value : head_value + 1]
    incoming = state_chain(
        gathered[:, :, :head_value], totals, list(range(seq_size)), seq_me
    )
    recurrent = local_out + jnp.einsum(
        "ntd,ned->nte", decayed_q.astype(jnp.bfloat16), incoming.astype(jnp.bfloat16),
        preferred_element_type=jnp.float32,
    )
    recurrent = from_heads(recurrent, batch).reshape(batch, seglen, -1, head_value)
    swish_gate = jnp.dot(hidden, swish_proj, preferred_element_type=jnp.float32).reshape(
        batch, seglen, -1, head_value
    )
    gated_f, head_back = jax.vjp(head_piece, recurrent, swish_gate, head_gain.astype(jnp.float32))
    gated = gated_f.astype(jnp.bfloat16).reshape(rows, value_width)
    mixer_part = jnp.dot(gated, output_proj, preferred_element_type=jnp.float32)
    middle_own = inputs_flat + lax.psum(mixer_part.astype(jnp.bfloat16), "tensor").astype(jnp.float32)
    hidden_two_own, norm_two_back = jax.vjp(root_norm, middle_own, feed_gain_f)
    hidden_two = hidden_two_own.astype(jnp.bfloat16)
    gate_pre = jnp.dot(hidden_two, feed_gate, preferred_element_type=jnp.float32)
    lift_pre = jnp.dot(hidden_two, feed_lift, preferred_element_type=jnp.float32)
    activation_f, feed_back = jax.vjp(feed_piece, gate_pre, lift_pre)
    activation = activation_f.astype(jnp.bfloat16)
    feed_part = jnp.dot(activation, feed_down, preferred_element_type=jnp.float32)
    mixed = (
        middle_own + lax.psum(feed_part.astype(jnp.bfloat16), "tensor").astype(jnp.float32)
    ).astype(jnp.bfloat16)
    mixed = mixed.reshape(batch, seglen, width)
    upstream = cotangent.astype(jnp.float32).reshape(rows, width)
    feed_out_grad = cotangent.reshape(rows, width)
    grad_feed_down = jnp.dot(activation.T, feed_out_grad, preferred_element_type=jnp.float32)
    activation_grad = jnp.dot(feed_out_grad, feed_down.T, preferred_element_type=jnp.float32)
    gate_pre_grad, lift_pre_grad = feed_back(activation_grad)
    gate_pre_grad = gate_pre_grad.astype(jnp.bfloat16)
    lift_pre_grad = lift_pre_grad.astype(jnp.bfloat16)
    grad_feed_gate = jnp.dot(hidden_two.T, gate_pre_grad, preferred_element_type=jnp.float32)
    grad_feed_lift = jnp.dot(hidden_two.T, lift_pre_grad, preferred_element_type=jnp.float32)
    hidden_two_part = jnp.dot(
        gate_pre_grad, feed_gate.T, preferred_element_type=jnp.float32
    ) + jnp.dot(lift_pre_grad, feed_lift.T, preferred_element_type=jnp.float32)
    two_grad_own = lax.psum(hidden_two_part.astype(jnp.bfloat16), "tensor").astype(jnp.float32)
    middle_norm_grad, grad_feed_gain = norm_two_back(two_grad_own)
    middle_grad_own = upstream + middle_norm_grad
    mixer_grad = middle_grad_own.astype(jnp.bfloat16)
    grad_output_proj = jnp.dot(gated.T, mixer_grad, preferred_element_type=jnp.float32)
    gated_grad = jnp.dot(mixer_grad, output_proj.T, preferred_element_type=jnp.float32).reshape(
        batch, seglen, -1, head_value
    )
    recurrent_grad, swish_grad, head_gain_part = head_back(gated_grad)
    swish_gate_grad = swish_grad.reshape(rows, value_width).astype(jnp.bfloat16)
    recurrent_grad = to_heads(recurrent_grad.reshape(batch, seglen, value_width), head_value)
    local_pull = jnp.einsum(
        "ntd,nte->ned", decayed_q.astype(jnp.bfloat16), recurrent_grad.astype(jnp.bfloat16),
        preferred_element_type=jnp.float32,
    )
    pulls = lax.all_gather(local_pull.astype(jnp.bfloat16), "seq").astype(jnp.float32)
    outgoing_grad = state_chain(pulls, totals, list(range(seq_size))[::-1], seq_me)
    queries_grad, keys_grad, values_grad, decays_grad = run_groups(
        backward_kernel,
        (rows_const, rowst_const),
        (
            queries,
            keylist,
            values,
            decays,
            recurrent_grad,
            states,
            offsets,
            incoming,
            outgoing_grad,
        ),
        (queries.shape, queries.shape, values.shape, queries.shape),
        2 * flops,
    )
    activated_grad = jnp.concatenate(
        [
            from_heads(queries_grad, batch) * scale,
            from_heads(keys_grad, batch),
            from_heads(values_grad, batch),
        ],
        -1,
    )
    log_decay_grad = from_heads(decays_grad, batch).reshape(rows, key_width)
    logit_grad = log_decay_grad * jax.nn.sigmoid(-decay_logit) / 16.0
    grad_decay_bias = jnp.sum(logit_grad, axis=0)
    grad_decay_up = jnp.dot(low_rank.T, logit_grad, precision=highest)
    low_rank_part = jnp.dot(logit_grad, decay_up.astype(jnp.float32).T, precision=highest)
    padded_grad, conv_grad = conv_back(activated_grad)
    returned = shifted(padded_grad[:, : conv_width - 1], "seq", -1)
    raw_grad = padded_grad[:, conv_width - 1 :]
    raw_grad = jnp.concatenate(
        [raw_grad[:, : seglen - conv_width + 1], raw_grad[:, seglen - conv_width + 1 :] + returned],
        1,
    )
    raw_grad = raw_grad.astype(jnp.bfloat16).reshape(rows, -1)
    query_grad_raw = raw_grad[:, :key_width]
    key_grad_raw = raw_grad[:, key_width : 2 * key_width]
    value_grad_raw = raw_grad[:, 2 * key_width :]
    grad_query_proj = jnp.dot(hidden.T, query_grad_raw, preferred_element_type=jnp.float32)
    grad_key_proj = jnp.dot(hidden.T, key_grad_raw, preferred_element_type=jnp.float32)
    grad_value_proj = jnp.dot(hidden.T, value_grad_raw, preferred_element_type=jnp.float32)
    grad_swish_proj = jnp.dot(hidden.T, swish_gate_grad, preferred_element_type=jnp.float32)
    hidden_part = (
        jnp.dot(query_grad_raw, query_proj.T, preferred_element_type=jnp.float32)
        + jnp.dot(key_grad_raw, key_proj.T, preferred_element_type=jnp.float32)
        + jnp.dot(value_grad_raw, value_proj.T, preferred_element_type=jnp.float32)
        + jnp.dot(swish_gate_grad, swish_proj.T, preferred_element_type=jnp.float32)
    )
    decay_down_f = decay_down.astype(jnp.float32)
    hidden_sum, low_rank_grad, grad_head_gain = (
        lax.psum(hidden_part.astype(jnp.bfloat16), "tensor").astype(jnp.float32),
        lax.psum(low_rank_part.astype(jnp.bfloat16), "tensor").astype(jnp.float32),
        lax.psum(head_gain_part.astype(jnp.bfloat16), "tensor").astype(jnp.float32),
    )
    hidden_grad = hidden_sum + jnp.dot(low_rank_grad, decay_down_f.T, precision=highest)
    grad_decay_down = jnp.dot(hidden.astype(jnp.float32).T, low_rank_grad, precision=highest)
    inputs_norm_grad, grad_attention_gain = norm_back(hidden_grad)
    tokens_grad = middle_grad_own + inputs_norm_grad
    tokens_grad = tokens_grad.reshape(batch, seglen, width)
    grad_query_conv = conv_grad[:, :key_width]
    grad_key_conv = conv_grad[:, key_width : 2 * key_width]
    grad_value_conv = conv_grad[:, 2 * key_width :]
    grad_query_proj, grad_key_proj, grad_value_proj, grad_swish_proj = split_sum(
        (grad_query_proj, grad_key_proj, grad_value_proj, grad_swish_proj)
    )
    (grad_output_proj,) = split_sum((grad_output_proj,))
    grad_feed_gate, grad_feed_lift = split_sum((grad_feed_gate, grad_feed_lift))
    (grad_feed_down,) = split_sum((grad_feed_down,))
    small = (
        grad_attention_gain,
        grad_query_conv,
        grad_key_conv,
        grad_value_conv,
        grad_decay_down,
        grad_decay_up,
        grad_decay_bias,
        grad_head_gain,
        grad_feed_gain,
    )
    flat = lax.psum(jnp.concatenate([x.reshape(-1) for x in small]), ("dp", "seq"))
    summed, start = [], 0
    for x in small:
        summed.append(flat[start : start + x.size].reshape(x.shape))
        start += x.size
    (
        grad_attention_gain,
        grad_query_conv,
        grad_key_conv,
        grad_value_conv,
        grad_decay_down,
        grad_decay_up,
        grad_decay_bias,
        grad_head_gain,
        grad_feed_gain,
    ) = summed
    return (
        mixed,
        tokens_grad,
        grad_attention_gain,
        grad_query_proj,
        grad_key_proj,
        grad_value_proj,
        grad_query_conv,
        grad_key_conv,
        grad_value_conv,
        grad_decay_down,
        grad_decay_up,
        grad_decay_bias,
        grad_swish_proj,
        grad_head_gain,
        grad_output_proj,
        grad_feed_gain,
        grad_feed_gate,
        grad_feed_lift,
        grad_feed_down,
    )


def solution(mesh):
    return jax.shard_map(
        on_device,
        mesh=mesh,
        in_specs=(
            P("dp", "seq", None),
            P("dp", "seq", None),
            P(),
            P(None, "tensor"),
            P(None, "tensor"),
            P(None, "tensor"),
            P(None, "tensor"),
            P(None, "tensor"),
            P(None, "tensor"),
            P(),
            P(None, "tensor"),
            P("tensor"),
            P(None, "tensor"),
            P(),
            P("tensor", None),
            P(),
            P(None, "tensor"),
            P(None, "tensor"),
            P("tensor", None),
        ),
        out_specs=(
            P("dp", "seq", None),
            P("dp", "seq", None),
            P(),
            P(None, "tensor"),
            P(None, "tensor"),
            P(None, "tensor"),
            P(None, "tensor"),
            P(None, "tensor"),
            P(None, "tensor"),
            P(),
            P(None, "tensor"),
            P("tensor"),
            P(None, "tensor"),
            P(),
            P("tensor", None),
            P(),
            P(None, "tensor"),
            P(None, "tensor"),
            P("tensor", None),
        ),
        check_vma=False,
    )
```

```python
import functools
import jax
import jax.numpy as jnp
import numpy as np
from jax import lax
from jax.experimental import pallas as pl
from jax.experimental.pallas import tpu as pltpu
from jax.sharding import PartitionSpec as P

HEAD_KEY = 128
CHUNK = 128


highest = lax.Precision.HIGHEST
epsilon = 1e-06


def shifted(x, axis, by):
    size = lax.axis_size(axis)
    pairs = [(i, i + by) for i in range(size) if 0 <= i + by < size]
    return lax.ppermute(x, axis, pairs)


def root_norm(values, gain):
    return values * lax.rsqrt(jnp.mean(values * values, axis=-1, keepdims=True) + epsilon) * gain


def convolve(padded, weight):
    width = weight.shape[0]
    length = padded.shape[1] - width + 1
    total = weight[0] * padded[:, 0:length]
    for offset in range(1, width):
        total = total + weight[offset] * padded[:, offset : offset + length]
    return jax.nn.silu(total)


def level_rows(chunk):
    index = np.arange(chunk)
    t, u = index[:, None], index[None, :]
    parts = []
    for level in range(chunk.bit_length() - 1):
        half = 1 << level
        last = (t // (2 * half)) * 2 * half + half - 1
        upper = (t > last) & (u > last) & (u <= t)
        lower = (t <= last) & (u > t) & (u <= last)
        parts.append(upper | lower)
    parts.append(u <= t)
    parts.append(u > t)
    return np.concatenate(parts, 0).astype(np.float32)


def dot(a, b, ca=1, cb=0):
    return lax.dot_general(
        a.astype(jnp.bfloat16),
        b.astype(jnp.bfloat16),
        (((ca,), (cb,)), ((), ())),
        preferred_element_type=jnp.float32,
    )


def chunk_factors(rows, decays):
    top = decays.astype(jnp.bfloat16)
    rest = (decays - top.astype(jnp.float32)).astype(jnp.bfloat16)
    both = dot(rows, jnp.concatenate([top, rest], 1))
    return both[:, :HEAD_KEY] + both[:, HEAD_KEY:]


def grids(chunk):
    t = lax.broadcasted_iota(jnp.int32, (chunk, chunk), 0)
    s = lax.broadcasted_iota(jnp.int32, (chunk, chunk), 1)
    r = lax.broadcasted_iota(jnp.int32, (chunk, HEAD_KEY), 0)
    return t, s, r


def chunk_scores(queries, keylist, factors, t, s, r, levels):
    chunk = queries.shape[0]
    mixed = t ^ s
    scores = jnp.where(
        t == s, jnp.sum(queries * keylist, axis=1, keepdims=True), 0.0
    )
    sides = []
    for level in range(levels):
        factor = factors[level * chunk : (level + 1) * chunk]
        side = (jnp.where(((r >> level) & 1) == 1, queries, keylist) * factor).astype(jnp.bfloat16)
        sides.append(side)
        product = dot(side, side, 1, 1)
        scores = jnp.where(((mixed >> level) == 1) & (t > s), product, scores)
    return scores, sides


def forward_kernel(rows_ref, q_ref, k_ref, v_ref, g_ref, o_ref, dq_ref, st_ref, off_ref, last_ref):
    chunk = rows_ref.shape[1]
    count = q_ref.shape[1] // chunk
    levels = chunk.bit_length() - 1
    rows = rows_ref[...]
    t, s, r = grids(chunk)
    state = jnp.zeros((v_ref.shape[2], HEAD_KEY), jnp.float32)
    offset = jnp.zeros((1, HEAD_KEY), jnp.float32)
    for c in range(count):
        part = pl.ds(c * chunk, chunk)
        queries, keylist, values = q_ref[0, part], k_ref[0, part], v_ref[0, part]
        raw = chunk_factors(rows, g_ref[0, part])
        factors = jnp.exp(raw)
        pre = factors[levels * chunk : (levels + 1) * chunk]
        suf = factors[(levels + 1) * chunk :]
        scores, _ = chunk_scores(queries, keylist, factors, t, s, r, levels)
        st_ref[0, c] = state
        off_ref[0, c] = jnp.broadcast_to(offset, (8, HEAD_KEY))
        queries_pre = queries * pre
        o_ref[0, part] = dot(scores, values) + dot(queries_pre, state, 1, 1)
        dq_ref[0, part] = queries_pre * jnp.exp(offset)
        state = state * pre[chunk - 1 :] + dot(values, keylist * suf, 0, 0)
        offset = offset + raw[(levels + 1) * chunk - 1 : (levels + 1) * chunk]
    off_ref[0, count] = jnp.broadcast_to(offset, (8, HEAD_KEY))
    last_ref[0] = state


def backward_kernel(
    rows_ref, rowst_ref, q_ref, k_ref, v_ref, g_ref, do_ref, st_ref, off_ref, inc_ref, out_ref,
    dq_ref, dk_ref, dv_ref, dg_ref,
):
    chunk = rows_ref.shape[1]
    count = q_ref.shape[1] // chunk
    levels = chunk.bit_length() - 1
    rows = rows_ref[...]
    rowst = rowst_ref[...]
    t, s, r = grids(chunk)
    mixed = t ^ s
    pull = out_ref[0]
    incoming = inc_ref[0]
    for c in reversed(range(count)):
        part = pl.ds(c * chunk, chunk)
        queries, keylist, values = q_ref[0, part], k_ref[0, part], v_ref[0, part]
        outer = do_ref[0, part]
        factors = jnp.exp(chunk_factors(rows, g_ref[0, part]))
        pre = factors[levels * chunk : (levels + 1) * chunk]
        suf = factors[(levels + 1) * chunk :]
        scores, sides = chunk_scores(queries, keylist, factors, t, s, r, levels)
        state = st_ref[0, c] + incoming * jnp.exp(off_ref[0, c][:1])
        lower = dot(outer, values, 1, 1)
        upper = dot(values, outer, 1, 1)
        both = jnp.where(t > s, lower, upper)
        own = jnp.sum(outer * values, axis=1, keepdims=True)
        dq = own * keylist
        dk = own * queries
        shares = []
        for level in range(levels):
            factor = factors[level * chunk : (level + 1) * chunk]
            back = dot(jnp.where((mixed >> level) == 1, both, 0.0), sides[level]) * factor
            bit = ((r >> level) & 1) == 1
            dq = dq + jnp.where(bit, back, 0.0)
            dk = dk + jnp.where(bit, 0.0, back)
            shares.append((back * jnp.where(bit, queries, keylist)).astype(jnp.bfloat16))
        from_state = dot(outer, state) * pre
        to_state = dot(values, pull) * suf
        dq = dq + from_state
        dk = dk + to_state
        shares.append((from_state * queries).astype(jnp.bfloat16))
        shares.append((to_state * keylist).astype(jnp.bfloat16))
        ending = pre[chunk - 1 :]
        whole = jnp.sum(state * pull, axis=0, keepdims=True) * ending
        dg = dot(rowst, jnp.concatenate(shares, 0)) + whole
        dq_ref[0, part] = dq
        dk_ref[0, part] = dk
        dg_ref[0, part] = dg
        dv_ref[0, part] = dot(scores, outer, 0, 0) + dot(keylist * suf, pull, 1, 1)
        pull = pull * ending + dot(outer, queries * pre, 0, 0)


def group_spec(shape):
    extra = len(shape) - 1
    return pl.BlockSpec((1,) + tuple(shape[1:]), lambda i: (i,) + (0,) * extra)


def whole_spec(shape):
    return pl.BlockSpec(tuple(shape), lambda i: (0,) * len(shape))


def run_groups(kernel, constants, arrays, outs, flops):
    return pl.pallas_call(
        kernel,
        grid=(arrays[0].shape[0],),
        in_specs=[whole_spec(a.shape) for a in constants] + [group_spec(a.shape) for a in arrays],
        out_specs=[group_spec(o) for o in outs],
        out_shape=[jax.ShapeDtypeStruct(o, jnp.float32) for o in outs],
        compiler_params=pltpu.CompilerParams(vmem_limit_bytes=48 * 1024 * 1024),
        cost_estimate=pl.CostEstimate(flops=flops, bytes_accessed=4000000, transcendentals=0),
    )(*constants, *arrays)


def state_chain(states, totals, order, me):
    carried = jnp.zeros_like(states[0])
    for j in order:
        follow = (j < me) if order[0] == 0 else (j > me)
        carried = jnp.where(follow, jnp.exp(totals[j]) * carried + states[j], carried)
    return carried


def to_heads(array, width):
    batch, length, channels = array.shape
    return (
        array.reshape(batch, length, channels // width, width)
        .transpose(0, 2, 1, 3)
        .reshape(batch * (channels // width), length, width)
    )


def from_heads(array, batch):
    groups, length, width = array.shape
    return (
        array.reshape(batch, groups // batch, length, width)
        .transpose(0, 2, 1, 3)
        .reshape(batch, length, groups // batch * width)
    )


def head_piece(outputs, gate, gain):
    return root_norm(outputs, gain) * jax.nn.silu(gate)


def feed_piece(gate_pre, lift_pre):
    return jax.nn.silu(gate_pre) * lift_pre


def peers_of(axes, sizes):
    index = lax.axis_index(axes[0])
    total = sizes[0]
    for axis, size in zip(axes[1:], sizes[1:]):
        index = index * size + lax.axis_index(axis)
        total = total * size

    def place(which):
        coords = {}
        for axis, size in reversed(list(zip(axes, sizes))):
            coords[axis] = lax.rem(which, size)
            which = which // size
        return coords

    others = [lax.rem(index + d, total) for d in range(1, total)]
    return index, [(other, place(other)) for other in others]


def greet(others):
    barrier = pltpu.get_barrier_semaphore()
    for _, place in others:
        pl.semaphore_signal(barrier, inc=1, device_id=place, device_id_type=pl.DeviceIdType.MESH)
    pl.semaphore_wait(barrier, len(others))


def remote(src, dst, send, recv, place):
    return pltpu.make_async_remote_copy(
        src_ref=src, dst_ref=dst, send_sem=send, recv_sem=recv,
        device_id=place, device_id_type=pl.DeviceIdType.MESH,
    )


def gather_kernel(axes, sizes, count, *refs):
    arrays, outs = refs[:count], refs[count : 2 * count]
    send, recv = refs[2 * count :]
    me, others = peers_of(axes, sizes)
    greet(others)
    copies = []
    for d, (_, place) in enumerate(others):
        for a in range(count):
            copies.append(remote(arrays[a], outs[a].at[me], send.at[a, d], recv.at[a, d], place))
            copies[-1].start()
    for a in range(count):
        outs[a][me] = arrays[a][...]
    for copy in copies:
        copy.wait()


def gather_direct(arrays, axes, sizes, ident):
    total = int(np.prod(sizes))
    vmem = pl.BlockSpec(memory_space=pltpu.VMEM)
    return pl.pallas_call(
        functools.partial(gather_kernel, axes, sizes, len(arrays)),
        out_shape=[jax.ShapeDtypeStruct((total,) + a.shape, a.dtype) for a in arrays],
        in_specs=[vmem] * len(arrays),
        out_specs=[vmem] * len(arrays),
        scratch_shapes=[pltpu.SemaphoreType.DMA((len(arrays), total - 1))] * 2,
        compiler_params=pltpu.CompilerParams(
            collective_id=ident, has_side_effects=True, vmem_limit_bytes=32 * 1024 * 1024
        ),
        cost_estimate=pl.CostEstimate(flops=0, bytes_accessed=12000000, transcendentals=0),
    )(*arrays)


def reduce_kernel(axes, sizes, count, *refs):
    arrays, outs, lands = refs[:count], refs[count : 2 * count], refs[2 * count : 3 * count]
    send_a, recv_a, send_b, recv_b = refs[3 * count :]
    me, others = peers_of(axes, sizes)
    total = len(others) + 1
    greet(others)

    def part(ref, which):
        rows = ref.shape[0] // total
        return ref.at[pl.ds(pl.multiple_of(which * rows, 16), rows)]

    first = [[] for _ in range(count)]
    for a in range(count):
        for d, (other, place) in enumerate(others):
            copy = remote(part(arrays[a], other), lands[a].at[d], send_a.at[a, d], recv_a.at[a, d], place)
            copy.start()
            first[a].append(copy)
    second = []
    for a in range(count):
        value = part(arrays[a], me)[...].astype(jnp.float32)
        for d in range(total - 1):
            first[a][d].wait_recv()
            value = value + lands[a][d].astype(jnp.float32)
        part(outs[a], me)[...] = value.astype(outs[a].dtype)
        for d, (_, place) in enumerate(others):
            copy = remote(part(outs[a], me), part(outs[a], me), send_b.at[a, d], recv_b.at[a, d], place)
            copy.start()
            second.append(copy)
    for a in range(count):
        for copy in first[a]:
            copy.wait_send()
    for copy in second:
        copy.wait()


def reduce_direct(arrays, axes, sizes, ident):
    total = int(np.prod(sizes))
    vmem = pl.BlockSpec(memory_space=pltpu.VMEM)
    count = len(arrays)
    return pl.pallas_call(
        functools.partial(reduce_kernel, axes, sizes, count),
        out_shape=[jax.ShapeDtypeStruct(a.shape, a.dtype) for a in arrays],
        in_specs=[vmem] * count,
        out_specs=[vmem] * count,
        scratch_shapes=[
            pltpu.VMEM((total - 1, a.shape[0] // total, a.shape[1]), a.dtype) for a in arrays
        ]
        + [pltpu.SemaphoreType.DMA((count, total - 1))] * 4,
        compiler_params=pltpu.CompilerParams(
            collective_id=ident, has_side_effects=True, vmem_limit_bytes=32 * 1024 * 1024
        ),
        cost_estimate=pl.CostEstimate(flops=0, bytes_accessed=60000000 * count, transcendentals=0),
    )(*arrays)


def split_sum(grads):
    sums = lax.psum(tuple(g.astype(jnp.bfloat16) for g in grads), ("dp", "seq"))
    return tuple(g.astype(jnp.float32) for g in sums)


def on_device(
    tokens,
    cotangent,
    attention_gain,
    query_proj,
    key_proj,
    value_proj,
    query_conv,
    key_conv,
    value_conv,
    decay_down,
    decay_up,
    decay_bias,
    swish_proj,
    head_gain,
    output_proj,
    feed_gain,
    feed_gate,
    feed_lift,
    feed_down,
):
    batch, seglen, width = tokens.shape
    rows = batch * seglen
    key_width = query_proj.shape[1]
    value_width = value_proj.shape[1]
    head_value = head_gain.shape[0]
    conv_width = query_conv.shape[0]
    scale = HEAD_KEY ** (-0.5)
    inputs_flat = tokens.astype(jnp.float32).reshape(rows, width)
    attention_gain_f = attention_gain.astype(jnp.float32)
    feed_gain_f = feed_gain.astype(jnp.float32)
    hidden_f, norm_back = jax.vjp(root_norm, inputs_flat, attention_gain_f)
    hidden = hidden_f.astype(jnp.bfloat16)
    query_raw = jnp.dot(hidden, query_proj, preferred_element_type=jnp.float32).astype(jnp.bfloat16)
    key_raw = jnp.dot(hidden, key_proj, preferred_element_type=jnp.float32).astype(jnp.bfloat16)
    value_raw = jnp.dot(hidden, value_proj, preferred_element_type=jnp.float32).astype(jnp.bfloat16)
    raw_rows = jnp.concatenate([query_raw, key_raw, value_raw], 1).reshape(batch, seglen, -1)
    edge_rows = shifted(raw_rows[:, seglen - conv_width + 1 :], "seq", 1)
    padded = jnp.concatenate([edge_rows, raw_rows], 1).astype(jnp.float32)
    conv_all = jnp.concatenate([query_conv, key_conv, value_conv], 1).astype(jnp.float32)
    activated, conv_back = jax.vjp(convolve, padded, conv_all)
    queries = to_heads(activated[..., :key_width] * scale, HEAD_KEY)
    keylist = to_heads(activated[..., key_width : 2 * key_width], HEAD_KEY)
    values = to_heads(activated[..., 2 * key_width :], head_value)
    low_rank = jnp.dot(hidden, decay_down, preferred_element_type=jnp.float32)
    decay_logit = jnp.dot(low_rank, decay_up.astype(jnp.float32), precision=highest) + decay_bias
    log_decay = jax.nn.log_sigmoid(decay_logit) / 16.0
    decays = to_heads(log_decay.reshape(batch, seglen, key_width), HEAD_KEY)
    groups = queries.shape[0]
    chunk = min(CHUNK, seglen)
    count = seglen // chunk
    row_table = level_rows(chunk)
    rows_const = jnp.asarray(row_table, jnp.bfloat16)
    rowst_const = jnp.asarray(row_table.T, jnp.bfloat16)
    flops = groups * seglen * 3000000
    local_out, decayed_q, states, offsets, local_state = run_groups(
        forward_kernel,
        (rows_const,),
        (queries, keylist, values, decays),
        (
            (groups, seglen, head_value),
            (groups, seglen, HEAD_KEY),
            (groups, count, head_value, HEAD_KEY),
            (groups, count + 1, 8, HEAD_KEY),
            (groups, head_value, HEAD_KEY),
        ),
        flops,
    )
    tensor_size = lax.axis_size("tensor")
    seq_size = lax.axis_size("seq")
    seq_me = lax.axis_index("seq")
    flat_state = local_state.astype(jnp.bfloat16).reshape(groups * head_value, HEAD_KEY)
    flat_total = offsets[:, count].reshape(groups * 8, HEAD_KEY)
    gathered, totals = gather_direct((flat_state, flat_total), ("seq",), (seq_size,), 1)
    gathered = gathered.reshape(seq_size, groups, head_value, HEAD_KEY).astype(jnp.float32)
    totals = totals.reshape(seq_size, groups, 8, HEAD_KEY)[:, :, :1]
    incoming = state_chain(gathered, totals, list(range(seq_size)), seq_me)
    recurrent = local_out + jnp.einsum(
        "ntd,ned->nte", decayed_q.astype(jnp.bfloat16), incoming.astype(jnp.bfloat16),
        preferred_element_type=jnp.float32,
    )
    recurrent = from_heads(recurrent, batch).reshape(batch, seglen, -1, head_value)
    swish_gate = jnp.dot(hidden, swish_proj, preferred_element_type=jnp.float32).reshape(
        batch, seglen, -1, head_value
    )
    gated_f, head_back = jax.vjp(head_piece, recurrent, swish_gate, head_gain.astype(jnp.float32))
    gated = gated_f.astype(jnp.bfloat16).reshape(rows, value_width)
    mixer_part = jnp.dot(gated, output_proj, preferred_element_type=jnp.float32)
    middle_own = inputs_flat + reduce_direct(
        (mixer_part.astype(jnp.bfloat16),), ("tensor",), (tensor_size,), 3
    )[0].astype(jnp.float32)
    hidden_two_own, norm_two_back = jax.vjp(root_norm, middle_own, feed_gain_f)
    hidden_two = hidden_two_own.astype(jnp.bfloat16)
    gate_pre = jnp.dot(hidden_two, feed_gate, preferred_element_type=jnp.float32)
    lift_pre = jnp.dot(hidden_two, feed_lift, preferred_element_type=jnp.float32)
    activation_f, feed_back = jax.vjp(feed_piece, gate_pre, lift_pre)
    activation = activation_f.astype(jnp.bfloat16)
    feed_part = jnp.dot(activation, feed_down, preferred_element_type=jnp.float32)
    upstream = cotangent.astype(jnp.float32).reshape(rows, width)
    feed_out_grad = cotangent.reshape(rows, width)
    grad_feed_down = jnp.dot(activation.T, feed_out_grad, preferred_element_type=jnp.float32)
    activation_grad = jnp.dot(feed_out_grad, feed_down.T, preferred_element_type=jnp.float32)
    gate_pre_grad, lift_pre_grad = feed_back(activation_grad)
    gate_pre_grad = gate_pre_grad.astype(jnp.bfloat16)
    lift_pre_grad = lift_pre_grad.astype(jnp.bfloat16)
    grad_feed_gate = jnp.dot(hidden_two.T, gate_pre_grad, preferred_element_type=jnp.float32)
    grad_feed_lift = jnp.dot(hidden_two.T, lift_pre_grad, preferred_element_type=jnp.float32)
    hidden_two_part = jnp.dot(
        gate_pre_grad, feed_gate.T, preferred_element_type=jnp.float32
    ) + jnp.dot(lift_pre_grad, feed_lift.T, preferred_element_type=jnp.float32)
    grad_feed_gate, grad_feed_lift, grad_feed_down = split_sum(
        (grad_feed_gate, grad_feed_lift, grad_feed_down)
    )
    two_grad_own = reduce_direct(
        (hidden_two_part.astype(jnp.bfloat16),), ("tensor",), (tensor_size,), 4
    )[0].astype(jnp.float32)
    middle_norm_grad, grad_feed_gain = norm_two_back(two_grad_own)
    middle_grad_own = upstream + middle_norm_grad
    mixer_grad = middle_grad_own.astype(jnp.bfloat16)
    grad_output_proj = jnp.dot(gated.T, mixer_grad, preferred_element_type=jnp.float32)
    gated_grad = jnp.dot(mixer_grad, output_proj.T, preferred_element_type=jnp.float32).reshape(
        batch, seglen, -1, head_value
    )
    recurrent_grad, swish_grad, head_gain_part = head_back(gated_grad)
    swish_gate_grad = swish_grad.reshape(rows, value_width).astype(jnp.bfloat16)
    recurrent_grad = to_heads(recurrent_grad.reshape(batch, seglen, value_width), head_value)
    local_pull = jnp.einsum(
        "ntd,nte->ned", decayed_q.astype(jnp.bfloat16), recurrent_grad.astype(jnp.bfloat16),
        preferred_element_type=jnp.float32,
    )
    flat_pull = local_pull.astype(jnp.bfloat16).reshape(groups * head_value, HEAD_KEY)
    (pulls,) = gather_direct((flat_pull,), ("seq",), (seq_size,), 2)
    pulls = pulls.reshape(seq_size, groups, head_value, HEAD_KEY).astype(jnp.float32)
    outgoing_grad = state_chain(pulls, totals, list(range(seq_size))[::-1], seq_me)
    queries_grad, keys_grad, values_grad, decays_grad = run_groups(
        backward_kernel,
        (rows_const, rowst_const),
        (
            queries,
            keylist,
            values,
            decays,
            recurrent_grad,
            states,
            offsets,
            incoming,
            outgoing_grad,
        ),
        (queries.shape, queries.shape, values.shape, queries.shape),
        2 * flops,
    )
    activated_grad = jnp.concatenate(
        [
            from_heads(queries_grad, batch) * scale,
            from_heads(keys_grad, batch),
            from_heads(values_grad, batch),
        ],
        -1,
    )
    log_decay_grad = from_heads(decays_grad, batch).reshape(rows, key_width)
    logit_grad = log_decay_grad * jax.nn.sigmoid(-decay_logit) / 16.0
    grad_decay_bias = jnp.sum(logit_grad, axis=0)
    grad_decay_up = jnp.dot(low_rank.T, logit_grad, precision=highest)
    low_rank_part = jnp.dot(logit_grad, decay_up.astype(jnp.float32).T, precision=highest)
    padded_grad, conv_grad = conv_back(activated_grad)
    returned = shifted(padded_grad[:, : conv_width - 1], "seq", -1)
    raw_grad = padded_grad[:, conv_width - 1 :]
    raw_grad = jnp.concatenate(
        [raw_grad[:, : seglen - conv_width + 1], raw_grad[:, seglen - conv_width + 1 :] + returned],
        1,
    )
    raw_grad = raw_grad.astype(jnp.bfloat16).reshape(rows, -1)
    query_grad_raw = raw_grad[:, :key_width]
    key_grad_raw = raw_grad[:, key_width : 2 * key_width]
    value_grad_raw = raw_grad[:, 2 * key_width :]
    grad_query_proj = jnp.dot(hidden.T, query_grad_raw, preferred_element_type=jnp.float32)
    grad_key_proj = jnp.dot(hidden.T, key_grad_raw, preferred_element_type=jnp.float32)
    grad_value_proj = jnp.dot(hidden.T, value_grad_raw, preferred_element_type=jnp.float32)
    grad_swish_proj = jnp.dot(hidden.T, swish_gate_grad, preferred_element_type=jnp.float32)
    hidden_part = (
        jnp.dot(query_grad_raw, query_proj.T, preferred_element_type=jnp.float32)
        + jnp.dot(key_grad_raw, key_proj.T, preferred_element_type=jnp.float32)
        + jnp.dot(value_grad_raw, value_proj.T, preferred_element_type=jnp.float32)
        + jnp.dot(swish_gate_grad, swish_proj.T, preferred_element_type=jnp.float32)
    )
    decay_down_f = decay_down.astype(jnp.float32)
    hidden_part = hidden_part + jnp.dot(low_rank_part, decay_down_f.T)
    decay_down_part = lax.dot_general(low_rank_part, hidden.astype(jnp.float32), (((0,), (0,)), ((), ())))
    rank = decay_down.shape[1]
    spare = 16 * tensor_size - rank - 1
    small_part = jnp.concatenate(
        [
            decay_down_part,
            jnp.pad(head_gain_part, (0, width - head_value))[None],
            jnp.zeros((spare, width), jnp.float32),
        ],
        0,
    )
    late = (grad_query_proj, grad_key_proj, grad_value_proj, grad_swish_proj, grad_output_proj)
    late, grad_feed_gate, grad_feed_lift, grad_feed_down = lax.optimization_barrier(
        (late, grad_feed_gate, grad_feed_lift, grad_feed_down)
    )
    grad_query_proj, grad_key_proj, grad_value_proj, grad_swish_proj, grad_output_proj = split_sum(late)
    hidden_sum, feed_sum, small_sum = reduce_direct(
        (
            hidden_part.astype(jnp.bfloat16),
            feed_part.astype(jnp.bfloat16),
            small_part.astype(jnp.bfloat16),
        ),
        ("tensor",),
        (tensor_size,),
        5,
    )
    hidden_grad = hidden_sum.astype(jnp.float32)
    mixed = (middle_own + feed_sum.astype(jnp.float32)).astype(jnp.bfloat16)
    mixed = mixed.reshape(batch, seglen, width)
    grad_decay_down = small_sum[:rank].astype(jnp.float32)
    grad_head_gain = small_sum[rank, :head_value].astype(jnp.float32)
    inputs_norm_grad, grad_attention_gain = norm_back(hidden_grad)
    tokens_grad = middle_grad_own + inputs_norm_grad
    tokens_grad = tokens_grad.reshape(batch, seglen, width)
    grad_query_conv = conv_grad[:, :key_width]
    grad_key_conv = conv_grad[:, key_width : 2 * key_width]
    grad_value_conv = conv_grad[:, 2 * key_width :]
    small = (
        grad_attention_gain,
        grad_query_conv,
        grad_key_conv,
        grad_value_conv,
        grad_decay_down,
        grad_decay_up,
        grad_decay_bias,
        grad_head_gain,
        grad_feed_gain,
    )
    flat = jnp.concatenate([x.reshape(-1).astype(jnp.bfloat16) for x in small])
    lines = -(-flat.size // (16 * width)) * 16
    flat = jnp.pad(flat, (0, lines * width - flat.size)).reshape(lines, width)
    (flat,) = gather_direct((flat,), ("dp", "seq"), (lax.axis_size("dp"), seq_size), 6)
    flat = jnp.sum(flat.astype(jnp.float32), axis=0).reshape(-1)
    summed, start = [], 0
    for x in small:
        summed.append(flat[start : start + x.size].reshape(x.shape))
        start += x.size
    (
        grad_attention_gain,
        grad_query_conv,
        grad_key_conv,
        grad_value_conv,
        grad_decay_down,
        grad_decay_up,
        grad_decay_bias,
        grad_head_gain,
        grad_feed_gain,
    ) = summed
    grad_decay_down = grad_decay_down.T
    return (
        mixed,
        tokens_grad,
        grad_attention_gain,
        grad_query_proj,
        grad_key_proj,
        grad_value_proj,
        grad_query_conv,
        grad_key_conv,
        grad_value_conv,
        grad_decay_down,
        grad_decay_up,
        grad_decay_bias,
        grad_swish_proj,
        grad_head_gain,
        grad_output_proj,
        grad_feed_gain,
        grad_feed_gate,
        grad_feed_lift,
        grad_feed_down,
    )


def solution(mesh):
    return jax.shard_map(
        on_device,
        mesh=mesh,
        in_specs=(
            P("dp", "seq", None),
            P("dp", "seq", None),
            P(),
            P(None, "tensor"),
            P(None, "tensor"),
            P(None, "tensor"),
            P(None, "tensor"),
            P(None, "tensor"),
            P(None, "tensor"),
            P(),
            P(None, "tensor"),
            P("tensor"),
            P(None, "tensor"),
            P(),
            P("tensor", None),
            P(),
            P(None, "tensor"),
            P(None, "tensor"),
            P("tensor", None),
        ),
        out_specs=(
            P("dp", "seq", None),
            P("dp", "seq", None),
            P(),
            P(None, "tensor"),
            P(None, "tensor"),
            P(None, "tensor"),
            P(None, "tensor"),
            P(None, "tensor"),
            P(None, "tensor"),
            P(),
            P(None, "tensor"),
            P("tensor"),
            P(None, "tensor"),
            P(),
            P("tensor", None),
            P(),
            P(None, "tensor"),
            P(None, "tensor"),
            P("tensor", None),
        ),
        check_vma=False,
    )
```
